32 devices in a mesh: dx: 8 (over z, y), dy: 4 (over x, core).
Axes of the slice: x: 2, y: 2, z: 4, core: 2. Of those that a mesh axis runs over, the one named last changes fastest.
Arguments:
- query_hidden: bfloat16 [512, 4096], P(('dx', 'dy')), as said below
- passage_hidden: bfloat16 [4096, 4096], P(('dx', 'dy')), as said below
- gain: float32 [4096], replicated, may hold values from 0.5 to 1.5
- hard_ids: int32 [512, 7], P(('dx', 'dy')), may hold values from 0 to 1023, as said below
- positive_ids: int32 [512], P(('dx', 'dy')), may hold values from 0 to 1023, as said below
Outputs:
- query_grad: bfloat16 [512, 4096], P(('dx', 'dy'))
- passage_grad: bfloat16 [4096, 4096], P(('dx', 'dy'))
- gain_grad: float32 [4096], replicated
- loss: float32 [], replicated
The draws below stay inside these ranges and needn't reach their ends.
Inputs may be any that keep to these rules, and one draw needn't show every extreme that they name: `query_hidden`: final-layer hidden states of order one. `passage_hidden`: final-layer hidden states of order one. `hard_ids`: the query of row r of device x of a group owns the 8 passage positions x * 128 + 8 * r to x * 128 + 8 * r + 7; its positive and its 7 hard negatives are these positions, each once. `positive_ids`: one of the query's own passage positions, as described for hard_ids.
All inputs are finite; a program needn't handle non-finite values.
Results may differ from the reference program's by a relative error of at most 0.017.
Values may be sent and summed in bfloat16 or wider, within the bound.
No kernel may reach another device: no remote copies, remote signals or barrier semaphores. Data moves between devices by JAX's collectives and lax.ppermute only.
A program may use at most 64 MiB of HBM per device.

```python
import jax
import jax.numpy as jnp
from jax import lax

D = 4096
Q_DEV = 16
HARD = 7
P_DEV = 128
GROUP_Q = 128
GROUP_P = 1024
QUERIES = 512
PASSAGES = 4096
N_DX = 8
N_DY = 4


def shared_rows(key):
    return jax.random.normal(key, (PASSAGES, D), jnp.float32)


def own_orders(key):
    key = jax.random.fold_in(key, 5)
    owned = HARD + 1
    rows = jnp.arange(QUERIES, dtype=jnp.int32)
    device = rows // Q_DEV
    local = rows % Q_DEV
    x_pos = device // N_DY
    start = x_pos * P_DEV + owned * local
    ranks = jax.random.randint(key, (QUERIES, owned), 0, 1 << 20, jnp.int32) * owned + jnp.arange(owned, dtype=jnp.int32)[None, :]
    order = jnp.argsort(ranks, axis=1).astype(jnp.int32)
    return start[:, None] + order


def draw_hard_ids(key, part):
    orders = own_orders(key)
    return orders[:, 1:]


def draw_positive_ids(key, part):
    orders = own_orders(key)
    return orders[:, 0]


def draw_query_hidden(key, part):
    key = jax.random.fold_in(key, 11)
    noise_key = jax.random.fold_in(key, 0)
    noise = jax.random.normal(noise_key, (QUERIES, D), jnp.float32)
    result = noise
    return result.astype(jnp.bfloat16)


def draw_passage_hidden(key, part):
    base = shared_rows(key)
    result = base
    return result.astype(jnp.bfloat16)


def setup_inputs(seed: int = 0) -> dict:
    seeds = jax.random.split(jax.random.key(seed), 6)
    return {
        "query_hidden": draw_query_hidden(jax.random.fold_in(seeds[5], 71), 0),
        "passage_hidden": draw_passage_hidden(jax.random.fold_in(seeds[5], 71), 0),
        "gain": jnp.clip(1.0 + 0.1 * jax.random.normal(seeds[2], (D,), jnp.float32), 0.5, 1.5),
        "hard_ids": draw_hard_ids(jax.random.fold_in(seeds[5], 71), 0),
        "positive_ids": draw_positive_ids(jax.random.fold_in(seeds[5], 71), 0),
    }


logit_scale = 250.0
hard_weight = 3.0

def embed(hidden, gain):
    values = hidden.astype(jnp.float32)
    inv_rms = lax.rsqrt(lax.optimization_barrier(jnp.mean(values * values, axis=-1, keepdims=True)) + 1e-05)
    unit = values * inv_rms
    normed = unit * gain
    inv_len = lax.rsqrt(lax.optimization_barrier(jnp.sum(normed * normed, axis=-1, keepdims=True)) + 1e-06)
    return ((normed * inv_len).astype(jnp.bfloat16), unit, normed, inv_len, inv_rms)

def backward(dembed, unit, normed, inv_len, inv_rms, gain):
    unit_embed = normed * inv_len
    dnormed = inv_len * (dembed - unit_embed * lax.optimization_barrier(jnp.sum(unit_embed * dembed, axis=-1, keepdims=True)))
    gain_part = lax.optimization_barrier(jnp.sum(dnormed * unit, axis=0))
    dunit = dnormed * gain
    grad = inv_rms * (dunit - unit * lax.optimization_barrier(jnp.mean(dunit * unit, axis=-1, keepdims=True)))
    return (grad.astype(jnp.bfloat16), gain_part)

def reference(query_hidden, passage_hidden, gain, hard_ids, positive_ids):
    q_emb, q_unit, q_normed, q_inv, q_rms = embed(query_hidden, gain)
    p_emb, p_unit, p_normed, p_inv, p_rms = embed(passage_hidden, gain)
    q_groups = q_emb.reshape(N_DX, N_DY, Q_DEV, D).transpose(1, 0, 2, 3).reshape(N_DY, GROUP_Q, D)
    p_groups = p_emb.reshape(N_DX, N_DY, P_DEV, D).transpose(1, 0, 2, 3).reshape(N_DY, GROUP_P, D)
    hard_groups = hard_ids.reshape(N_DX, N_DY, Q_DEV, HARD).transpose(1, 0, 2, 3).reshape(N_DY, GROUP_Q, HARD)
    pos_groups = positive_ids.reshape(N_DX, N_DY, Q_DEV).transpose(1, 0, 2).reshape(N_DY, GROUP_Q)
    col_ids = jnp.arange(GROUP_P, dtype=jnp.int32)

    def step(loss_total, item):
        q_rows, p_rows, hard_rows, pos_rows = item
        scores = logit_scale * lax.dot_general(q_rows, p_rows, (((1,), (1,)), ((), ())), preferred_element_type=jnp.float32)
        counts = jnp.zeros(scores.shape, jnp.float32)
        for k in range(HARD):
            counts = counts + (hard_rows[:, k:k + 1] == col_ids[None, :]).astype(jnp.float32)
        weights = 1.0 + hard_weight * counts
        is_pos = pos_rows[:, None] == col_ids[None, :]
        top = lax.optimization_barrier(jnp.max(scores, axis=1, keepdims=True))
        total = lax.optimization_barrier(jnp.sum(weights * jnp.exp(scores - top), axis=1, keepdims=True))
        log_total = top + jnp.log(total)
        pos_score = lax.optimization_barrier(jnp.sum(jnp.where(is_pos, scores, 0.0), axis=1))
        dscore = (weights * jnp.exp(scores - log_total) - is_pos.astype(jnp.float32)).astype(jnp.bfloat16)
        grouped = dscore.astype(jnp.float32).reshape(GROUP_Q, N_DX, P_DEV)
        p_blocks = p_rows.astype(jnp.float32).reshape(N_DX, P_DEV, D)
        dq_terms = logit_scale * jnp.einsum('qxp,xpd->qxd', grouped, p_blocks)
        dq_terms = lax.optimization_barrier(dq_terms.astype(jnp.bfloat16)).astype(jnp.float32)
        dq_rows = lax.optimization_barrier(jnp.sum(dq_terms, axis=1))
        dp_rows = logit_scale * lax.dot_general(dscore, q_rows, (((0,), (0,)), ((), ())), preferred_element_type=jnp.float32)
        loss_total = loss_total + jnp.sum(log_total[:, 0] - pos_score)
        return (loss_total, (dq_rows, dp_rows))
    loss, (dq_stack, dp_stack) = lax.scan(step, jnp.zeros((), jnp.float32), (q_groups, p_groups, hard_groups, pos_groups))
    dq_all = dq_stack.reshape(N_DY, N_DX, Q_DEV, D).transpose(1, 0, 2, 3).reshape(QUERIES, D)
    dp_all = dp_stack.reshape(N_DY, N_DX, P_DEV, D).transpose(1, 0, 2, 3).reshape(PASSAGES, D)
    query_grad, q_gain = backward(dq_all, q_unit, q_normed, q_inv, q_rms, gain)
    passage_grad, p_gain = backward(dp_all, p_unit, p_normed, p_inv, p_rms, gain)
    return (query_grad, passage_grad, q_gain + p_gain, loss)
```

```python
import functools

import jax
import jax.numpy as jnp
from jax import lax
from jax.experimental import pallas as pl
from jax.experimental.pallas import tpu as pltpu
from jax.sharding import PartitionSpec as P

logit_scale = 250.0
hard_weight = 3.0
rms_eps = 1e-05
len_eps = 1e-06
chunk = 512
piece = 256
vmem_bytes = 14 * 2**20

VMEM = pl.BlockSpec(memory_space=pltpu.VMEM)
SMEM = pl.BlockSpec(memory_space=pltpu.SMEM)
HBM = pl.BlockSpec(memory_space=pltpu.HBM)


def swap(value, axis, size, k):
    return lax.ppermute(value, axis, [(i, i ^ k) for i in range(size)])


def gather_blocks(own, axis, size, before):
    bits = [1 << b for b in reversed(range(size.bit_length() - 1))]
    first = [swap(own, axis, size, bit) for bit in bits]
    first[-1], first[0], before = lax.optimization_barrier((first[-1], first[0], before))
    blocks = {0: own}
    for bit, block in zip(bits, first):
        for j in sorted(blocks):
            blocks[j | bit] = swap(blocks[j], axis, size, bit) if j else block
    return [blocks[j] for j in range(size)], before


def spread(value, axis, size, first):
    return [value] + [swap(value, axis, size, first * k) for k in range(1, 4) if first * k < size]


def call(kernel, name, out, args, flops=0, **kw):
    moved = sum(a.size * a.dtype.itemsize for a in args)
    moved += sum(o.size * o.dtype.itemsize for o in jax.tree.leaves(out))
    limit = vmem_bytes + 2 * moved if moved > vmem_bytes // 2 else vmem_bytes
    return pl.pallas_call(
        kernel,
        out_shape=out,
        name=name,
        compiler_params=pltpu.CompilerParams(vmem_limit_bytes=limit),
        cost_estimate=pl.CostEstimate(flops=flops, bytes_accessed=moved, transcendentals=0),
        **kw,
    )(*args)


def row_scales(hidden, gain, rows):
    width = hidden.shape[1]
    squares = jnp.zeros((16, chunk), jnp.float32)
    scaled = jnp.zeros((16, chunk), jnp.float32)
    for c in range(0, width, chunk):
        h = hidden[rows, c : c + chunk].astype(jnp.float32)
        hg = h * gain[:, c : c + chunk]
        squares = squares + h * h
        scaled = scaled + hg * hg
    inv_rms = lax.rsqrt(jnp.sum(squares, axis=1, keepdims=True) / width + rms_eps)
    total = jnp.sum(scaled, axis=1, keepdims=True) * (inv_rms * inv_rms)
    return inv_rms, lax.rsqrt(total + len_eps)


def embed_rows(hidden, gain, out, inv_rms, inv_len, rows, to):
    scale = inv_rms * inv_len
    for c in range(0, hidden.shape[1], chunk):
        h = hidden[rows, c : c + chunk].astype(jnp.float32)
        out[to, c : c + chunk] = (h * gain[:, c : c + chunk] * scale).astype(jnp.bfloat16)


def embed_block(block, gain, out, to):
    rows = slice(0, block.shape[0])
    embed_rows(block, gain, out, *row_scales(block, gain, rows), rows, to)


def embed_kernel(hidden, own, gain, out, rms, length, queries):
    @pl.loop(0, hidden.shape[0] // 16)
    def _(i):
        rows = pl.ds(pl.multiple_of(i * 16, 16), 16)
        inv_rms, inv_len = row_scales(hidden, gain, rows)
        embed_rows(hidden, gain, out, inv_rms, inv_len, rows, rows)
        rms[rows, :] = inv_rms
        length[rows, :] = inv_len

    embed_block(own, gain, queries, slice(0, own.shape[0]))


def early_kernel(gain, blocks, queries):
    for i, block in enumerate(blocks):
        q_dev = block.shape[0]
        embed_block(block, gain, queries, slice(i * q_dev, (i + 1) * q_dev))


def masks(x_index, ids, shape):
    hard = ids.shape[0] - 1
    position = x_index * shape[0] + lax.broadcasted_iota(jnp.int32, shape, 0)
    counts = jnp.zeros(shape, jnp.float32)
    for k in range(hard):
        counts = counts + (ids[k : k + 1, :] == position).astype(jnp.float32)
    is_pos = ids[hard : hard + 1, :] == position
    return 1.0 + hard_weight * counts, is_pos.astype(jnp.float32)


def score_kernel(
    early, late, x_ref, ids, passages, gain, own, early_queries, blocks, scores, stats, queries
):
    q_dev = blocks[0].shape[0]
    span = lambda j: slice(j * q_dev, (j + 1) * q_dev)
    queries[span(0)] = own[...]
    for i, j in enumerate(early):
        queries[span(j)] = early_queries[span(i)]
    for i, j in enumerate(late):
        embed_block(blocks[i], gain, queries, span(j))
    s = logit_scale * lax.dot_general(
        passages[...], queries[...], (((1,), (1,)), ((), ())), preferred_element_type=jnp.float32
    )
    scores[...] = s
    weights, _ = masks(x_ref[0], ids[...], s.shape)
    top = jnp.max(s, axis=0, keepdims=True)
    stats[0] = top
    stats[1] = jnp.sum(weights * jnp.exp(s - top), axis=0, keepdims=True)


def turn(values, q_dev, bit, device_bit):
    width = values.shape[1]
    block = lax.broadcasted_iota(jnp.int32, values.shape, 1) // q_dev
    up = pltpu.roll(values, bit * q_dev, 1)
    down = pltpu.roll(values, width - bit * q_dev, 1)
    return jnp.where(device_bit, jnp.where(block & bit == 0, down, up), values)


def columns(rows):
    width = rows[0].shape[1]
    rows = rows + [jnp.zeros((128 - len(rows), width), jnp.float32)]
    return jnp.transpose(jnp.concatenate(rows, axis=0))


def term_kernel(x_ref, ids, stats, scores, passages, send_far, send_near, keep_far, keep_near):
    s = scores[...]
    half, q_dev, width = keep_near.shape
    tops = stats[0]
    other = lax.broadcasted_iota(jnp.int32, tops.shape, 0) == 1
    top = jnp.max(turn(tops, q_dev, 1, other), axis=0, keepdims=True)
    weights, _ = masks(x_ref[0], ids[...], s.shape)
    part = jnp.transpose(weights * jnp.exp(s - top)).astype(jnp.bfloat16)
    for c in range(0, width, chunk):
        cols = slice(c, c + chunk)
        t = jnp.dot(part, passages[:, cols], preferred_element_type=jnp.float32)
        t = (logit_scale * t).astype(jnp.bfloat16)
        for j in range(4 * half):
            near = j < 2 * half
            if j % 2:
                out = send_near if near else send_far
            else:
                out = keep_near if near else keep_far
            out[j // 2 % half, :, cols] = t[j * q_dev : (j + 1) * q_dev]


def gain_kernel(
    x_ref, ids, stats, scores, queries, passages, gain,
    dscore, along_out, gain_part, dq_own, scales, loss,
):
    blocks, group_q = stats.shape[1:]
    q_dev, width = dq_own.shape
    tops, sums = stats[0], stats[1]
    device = lax.broadcasted_iota(jnp.int32, tops.shape, 0)
    bit = 1
    while bit < blocks:
        tops = turn(tops, q_dev, bit, device & bit != 0)
        sums = turn(sums, q_dev, bit, device & bit != 0)
        bit *= 2
    top = jnp.max(tops, axis=0, keepdims=True)
    total = jnp.sum(sums * jnp.exp(tops - top), axis=0, keepdims=True)
    log_total = top + jnp.log(total)
    s = scores[...]
    weights, is_pos = masks(x_ref[0], ids[...], s.shape)
    d = (weights * jnp.exp(s - log_total) - is_pos).astype(jnp.bfloat16)
    wide = d.astype(jnp.float32)
    dscore[...] = d
    d_rows = jnp.transpose(wide).astype(jnp.bfloat16)
    ds = wide * s
    along_p = jnp.sum(ds, axis=1, keepdims=True)
    along_out[...] = along_p
    own = lax.broadcasted_iota(jnp.int32, (1, group_q), 1) < q_dev
    value = jnp.sum(jnp.where(own, log_total, 0.0)) - jnp.sum(is_pos * s)
    loss[...] = jnp.full(loss.shape, value, jnp.float32)
    pairs = jnp.exp(jnp.maximum(tops, pltpu.roll(tops, blocks - 1, 0)) - log_total)
    by = [pairs[j : j + 1] for j in range(0, blocks, 2)]
    by = columns(by + [jnp.sum(ds, axis=0, keepdims=True)])
    scales[...] = by[:q_dev]
    along_q = by[:, blocks // 2 : blocks // 2 + 1]

    for c in range(0, width, piece):
        cols = slice(c, c + piece)
        q, p = queries[:, cols], passages[:, cols]
        dq = logit_scale * jnp.dot(d_rows, p, preferred_element_type=jnp.float32)
        dq_own[:, cols] = dq[:q_dev]
        q, p = q.astype(jnp.float32), p.astype(jnp.float32)
        part = jnp.sum(q * (2.0 * dq - q * along_q), axis=0, keepdims=True)
        part = part - jnp.sum(p * (p * along_p), axis=0, keepdims=True)
        gain_part[:, cols] = part / gain[:, cols]


def grad_kernel(dscore, along, queries, hidden, gain, rms, length, grad_hbm, grad, sems):
    width = hidden.shape[1]
    r, inv, along_p = rms[...], length[...], along[...]
    d = dscore[...]
    by_dp = logit_scale * inv * r
    by_hg = inv * inv * r * r * along_p
    by_h = r * r * along_p * (inv * inv) * (len_eps / width)
    store = []
    for i, c in enumerate(range(0, width, piece)):
        cols = slice(c, c + piece)
        q, g = queries[:, cols], gain[:, cols]
        dp = jnp.dot(d, q, preferred_element_type=jnp.float32)
        h = hidden[:, cols].astype(jnp.float32)
        dnormed = by_dp * dp - by_hg * (h * g)
        grad[:, cols] = (dnormed * g - by_h * h).astype(jnp.bfloat16)
        done = pl.ds(c, piece)
        store.append(pltpu.make_async_copy(grad.at[:, done], grad_hbm.at[:, done], sems.at[i]))
        store[i].start()
    for copy in store:
        copy.wait()


def gain_sum_kernel(smalls, gain_grad, loss):
    small = smalls[0][...]
    for other in smalls[1:]:
        small = small + other[...]
    gain_grad[...] = small[:, : gain_grad.shape[1]]
    loss[...] = small[:, gain_grad.shape[1] : gain_grad.shape[1] + 1]


def query_grad_kernel(terms, dq_own, scales, hidden, gain, grad, dq):
    rows, width = hidden.shape
    r, inv = row_scales(hidden, gain, slice(0, 16))
    by = scales[...]
    along = jnp.zeros((rows, chunk), jnp.float32)
    for c in range(0, width, chunk):
        cols = slice(c, c + chunk)
        total = dq_own[:, cols]
        for j, term in enumerate(terms):
            total = total + term[:, cols].astype(jnp.float32) * by[:, j : j + 1]
        dq[:, cols] = total
        along = along + total * (hidden[:, cols].astype(jnp.float32) * gain[:, cols])
    along = jnp.sum(along, axis=1, keepdims=True) * (r * inv)
    mean = along * (inv * inv) * (len_eps / width)
    for c in range(0, width, chunk):
        cols = slice(c, c + chunk)
        h = hidden[:, cols].astype(jnp.float32)
        g = gain[:, cols]
        dnormed = inv * dq[:, cols] - (inv * inv * r * along) * (h * g)
        grad[:, cols] = (r * (dnormed * g) - (r * r * mean) * h).astype(jnp.bfloat16)


def on_device(n_dx, n_dy, query_hidden, passage_hidden, gain, hard_ids, positive_ids):
    q_dev, width = query_hidden.shape
    p_dev = passage_hidden.shape[0]
    group_q = n_dx * q_dev
    shape = jax.ShapeDtypeStruct
    bf16, f32 = jnp.bfloat16, jnp.float32
    gain = gain.reshape(1, width)
    x_index = lax.axis_index("dx").reshape(1)
    ids = jnp.concatenate([hard_ids, positive_ids[:, None]], axis=1).T
    ids = jnp.pad(ids, ((0, 0), (0, group_q - q_dev)), constant_values=-1)

    column, own = shape((p_dev, 1), f32), shape((q_dev, width), bf16)
    p_emb, p_rms, p_len, own_queries = call(
        embed_kernel, "embed", (shape((p_dev, width), bf16), column, column, own),
        (passage_hidden, query_hidden, gain), in_specs=[VMEM] * 3, out_specs=(VMEM,) * 4,
    )
    q_blocks, p_len = gather_blocks(query_hidden, "dx", n_dx, p_len)
    late = [j for j in range(n_dx) if j % 2 and j > 1]
    early = [j for j in range(1, n_dx) if j not in late]
    early_queries = call(
        lambda g, *refs: early_kernel(g, refs[:-1], refs[-1]), "early_queries",
        shape((len(early) * q_dev, width), bf16), (gain, *[q_blocks[j] for j in early]),
        in_specs=[VMEM] * (1 + len(early)), out_specs=VMEM,
    )
    macs = group_q * p_dev * width
    scores, stats, q_group = call(
        lambda x, i, p, g, o, e, *refs: score_kernel(
            early, late, x, i, p, g, o, e, refs[: len(late)], *refs[len(late) :]
        ), "scores",
        (shape((p_dev, group_q), f32), shape((2, 1, group_q), f32), shape((group_q, width), bf16)),
        (x_index, ids, p_emb, gain, own_queries, early_queries, *[q_blocks[j] for j in late]),
        flops=2 * macs, in_specs=[SMEM] + [VMEM] * (5 + len(late)), out_specs=(VMEM,) * 3,
    )
    half = n_dx // 4
    terms = shape((half, q_dev, width), bf16)
    stats = jnp.concatenate([stats, swap(stats, "dx", n_dx, 1)], axis=1)
    send_far, send_near, keep_far, keep_near = call(
        term_kernel, "query_terms", (terms,) * 4, (x_index, ids, stats, scores, p_emb),
        flops=2 * macs, in_specs=[SMEM] + [VMEM] * 4, out_specs=(VMEM,) * 4,
    )
    stats, send_far, send_near = lax.optimization_barrier((stats, send_far, send_near))
    far, near = swap(send_far, "dx", n_dx, 1), swap(send_near, "dx", n_dx, 1)
    stage = 2
    while stage < n_dx:
        stats = jnp.concatenate(spread(stats, "dx", n_dx, stage), axis=1)
        stage *= 4
    stats, far = lax.optimization_barrier((stats, far))
    far = far + keep_far
    far = [swap(far[i], "dx", n_dx, 2 * (half + i)) for i in range(half)]

    dscore, along, gain_part, dq_own, scales, loss = call(
        gain_kernel, "gain_part",
        (shape((p_dev, group_q), bf16), shape((p_dev, 1), f32), shape((1, width), f32),
         shape((q_dev, width), f32), shape((q_dev, 128), f32), shape((1, 128), f32)),
        (x_index, ids, stats, scores, q_group, p_emb, gain),
        flops=2 * macs, in_specs=[SMEM] + [VMEM] * 6, out_specs=(VMEM,) * 6,
    )
    passage_grad = call(
        grad_kernel, "passage_grad", shape((p_dev, width), bf16),
        (dscore, along, q_group, passage_hidden, gain, p_rms, p_len), flops=2 * macs,
        in_specs=[VMEM] * 7, out_specs=HBM,
        scratch_shapes=[pltpu.VMEM((p_dev, width), bf16),
                        pltpu.SemaphoreType.DMA((width // piece,))],
    )
    small = jnp.concatenate([gain_part, loss], axis=1)
    stage = 1
    while stage < n_dy:
        small = sum(spread(small, "dy", n_dy, stage))
        stage *= 4
    near, _ = lax.optimization_barrier((near, small))
    pairs = near + keep_near
    terms = [near[0]] + [swap(pairs[i], "dx", n_dx, 2 * i) for i in range(1, half)] + far
    bit = 1
    while 2 * bit < n_dx:
        small = small + swap(small, "dx", n_dx, bit)
        bit *= 2
    smalls = [small, swap(small, "dx", n_dx, bit)]
    n = len(terms)
    query_grad = call(
        lambda *refs: query_grad_kernel(refs[:n], *refs[n:]),
        "query_grad", shape((q_dev, width), bf16), (*terms, dq_own, scales, query_hidden, gain),
        in_specs=[VMEM] * (n + 4), out_specs=VMEM,
        scratch_shapes=[pltpu.VMEM((q_dev, width), f32)],
    )
    *smalls, _ = lax.optimization_barrier((*smalls, query_grad))
    gain_grad, loss = call(
        lambda *refs: gain_sum_kernel(refs[:-2], *refs[-2:]), "gain_sum",
        (shape((1, width), f32), shape((1, 1), f32)), smalls,
        in_specs=[VMEM] * len(smalls), out_specs=(VMEM,) * 2,
    )
    return (query_grad, passage_grad, gain_grad.reshape(width), loss.reshape(()))


def solution(mesh):
    n_dx, n_dy = mesh.shape["dx"], mesh.shape["dy"]
    placed = (
        P(("dx", "dy"), None),
        P(("dx", "dy"), None),
        P(),
        P(("dx", "dy"), None),
        P(("dx", "dy")),
    )
    return jax.shard_map(
        functools.partial(on_device, n_dx, n_dy),
        mesh=mesh,
        in_specs=placed,
        out_specs=(P(("dx", "dy"), None), P(("dx", "dy"), None), P(), P()),
        check_vma=False,
    )
```

```python
import functools

import jax
import jax.numpy as jnp
from jax import lax
from jax.experimental import pallas as pl
from jax.experimental.pallas import tpu as pltpu
from jax.sharding import PartitionSpec as P

logit_scale = 250.0
hard_weight = 3.0
rms_eps = 1e-05
len_eps = 1e-06
chunk = 512
piece = 256
vmem_bytes = 14 * 2**20

VMEM = pl.BlockSpec(memory_space=pltpu.VMEM)
SMEM = pl.BlockSpec(memory_space=pltpu.SMEM)
HBM = pl.BlockSpec(memory_space=pltpu.HBM)


def swap(value, axis, size, k):
    return lax.ppermute(value, axis, [(i, i ^ k) for i in range(size)])


def gather_blocks(own, axis, size, before):
    bits = [1 << b for b in reversed(range(size.bit_length() - 1))]
    first = [swap(own, axis, size, bit) for bit in bits]
    first[-1], first[0], before = lax.optimization_barrier((first[-1], first[0], before))
    blocks = {0: own}
    blocks.update(zip(bits, first))
    for bit in bits[1:]:
        for j in range(1, size):
            if j & bit and j not in blocks and j ^ bit in blocks:
                if bit > 1 or j & bits[0]:
                    blocks[j] = swap(blocks[j ^ bit], axis, size, bit)
    return [blocks[j] for j in range(size)], before


def spread(value, axis, size, first):
    return [value] + [swap(value, axis, size, first * k) for k in range(1, 4) if first * k < size]


def call(kernel, name, out, args, flops=0, **kw):
    moved = sum(a.size * a.dtype.itemsize for a in args)
    moved += sum(o.size * o.dtype.itemsize for o in jax.tree.leaves(out))
    limit = vmem_bytes + 2 * moved if moved > vmem_bytes // 2 else vmem_bytes
    return pl.pallas_call(
        kernel,
        out_shape=out,
        name=name,
        compiler_params=pltpu.CompilerParams(vmem_limit_bytes=limit),
        cost_estimate=pl.CostEstimate(flops=flops, bytes_accessed=moved, transcendentals=0),
        **kw,
    )(*args)


def row_scales(hidden, gain, rows):
    width = hidden.shape[1]
    squares = jnp.zeros((16, chunk), jnp.float32)
    scaled = jnp.zeros((16, chunk), jnp.float32)
    for c in range(0, width, chunk):
        h = hidden[rows, c : c + chunk].astype(jnp.float32)
        hg = h * gain[:, c : c + chunk]
        squares = squares + h * h
        scaled = scaled + hg * hg
    inv_rms = lax.rsqrt(jnp.sum(squares, axis=1, keepdims=True) / width + rms_eps)
    total = jnp.sum(scaled, axis=1, keepdims=True) * (inv_rms * inv_rms)
    return inv_rms, lax.rsqrt(total + len_eps)


def embed_rows(hidden, gain, out, inv_rms, inv_len, rows, to):
    scale = inv_rms * inv_len
    for c in range(0, hidden.shape[1], chunk):
        h = hidden[rows, c : c + chunk].astype(jnp.float32)
        out[to, c : c + chunk] = (h * gain[:, c : c + chunk] * scale).astype(jnp.bfloat16)


def embed_block(block, gain, out, to):
    rows = slice(0, block.shape[0])
    embed_rows(block, gain, out, *row_scales(block, gain, rows), rows, to)


def embed_kernel(hidden, own, gain, out, rms, length, queries):
    @pl.loop(0, hidden.shape[0] // 16)
    def _(i):
        rows = pl.ds(pl.multiple_of(i * 16, 16), 16)
        inv_rms, inv_len = row_scales(hidden, gain, rows)
        embed_rows(hidden, gain, out, inv_rms, inv_len, rows, rows)
        rms[rows, :] = inv_rms
        length[rows, :] = inv_len

    embed_block(own, gain, queries, slice(0, own.shape[0]))


def early_kernel(gain, blocks, queries):
    for i, block in enumerate(blocks):
        q_dev = block.shape[0]
        embed_block(block, gain, queries, slice(i * q_dev, (i + 1) * q_dev))


def masks(x_index, ids, shape):
    hard = ids.shape[0] - 1
    position = x_index * shape[0] + lax.broadcasted_iota(jnp.int32, shape, 0)
    counts = jnp.zeros(shape, jnp.float32)
    for k in range(hard):
        counts = counts + (ids[k : k + 1, :] == position).astype(jnp.float32)
    is_pos = ids[hard : hard + 1, :] == position
    return 1.0 + hard_weight * counts, is_pos.astype(jnp.float32)


def score_kernel(
    early, late, x_ref, ids, passages, gain, own, early_queries, blocks, scores, stats, queries
):
    q_dev = blocks[0].shape[0]
    span = lambda j: slice(j * q_dev, (j + 1) * q_dev)
    queries[span(0)] = own[...]
    for i, j in enumerate(early):
        queries[span(j)] = early_queries[span(i)]
    for i, j in enumerate(late):
        embed_block(blocks[i], gain, queries, span(j))
    s = logit_scale * lax.dot_general(
        passages[...], queries[...], (((1,), (1,)), ((), ())), preferred_element_type=jnp.float32
    )
    scores[...] = s
    weights, _ = masks(x_ref[0], ids[...], s.shape)
    top = jnp.max(s, axis=0, keepdims=True)
    stats[0] = top
    stats[1] = jnp.sum(weights * jnp.exp(s - top), axis=0, keepdims=True)


def turn(values, q_dev, bit, device_bit):
    width = values.shape[1]
    block = lax.broadcasted_iota(jnp.int32, values.shape, 1) // q_dev
    up = pltpu.roll(values, bit * q_dev, 1)
    down = pltpu.roll(values, width - bit * q_dev, 1)
    return jnp.where(device_bit, jnp.where(block & bit == 0, down, up), values)


def columns(rows):
    width = rows[0].shape[1]
    rows = rows + [jnp.zeros((128 - len(rows), width), jnp.float32)]
    return jnp.transpose(jnp.concatenate(rows, axis=0))


def term_kernel(x_ref, ids, stats, scores, passages, send_far, send_near, keep_far, keep_near):
    s = scores[...]
    half, q_dev, width = keep_near.shape
    tops = stats[0]
    other = lax.broadcasted_iota(jnp.int32, tops.shape, 0) == 1
    top = jnp.max(turn(tops, q_dev, 1, other), axis=0, keepdims=True)
    weights, _ = masks(x_ref[0], ids[...], s.shape)
    part = jnp.transpose(weights * jnp.exp(s - top)).astype(jnp.bfloat16)
    for c in range(0, width, chunk):
        cols = slice(c, c + chunk)
        t = jnp.dot(part, passages[:, cols], preferred_element_type=jnp.float32)
        t = (logit_scale * t).astype(jnp.bfloat16)
        for j in range(4 * half):
            near = j < 2 * half
            if j % 2:
                out = send_near if near else send_far
            else:
                out = keep_near if near else keep_far
            out[j // 2 % half, :, cols] = t[j * q_dev : (j + 1) * q_dev]


def gain_kernel(
    x_ref, ids, stats, scores, queries, passages, gain,
    dscore, along_out, gain_part, dq_own, scales, loss,
):
    blocks, group_q = stats.shape[1:]
    q_dev, width = dq_own.shape
    tops, sums = stats[0], stats[1]
    device = lax.broadcasted_iota(jnp.int32, tops.shape, 0)
    bit = 1
    while bit < blocks:
        tops = turn(tops, q_dev, bit, device & bit != 0)
        sums = turn(sums, q_dev, bit, device & bit != 0)
        bit *= 2
    top = jnp.max(tops, axis=0, keepdims=True)
    total = jnp.sum(sums * jnp.exp(tops - top), axis=0, keepdims=True)
    log_total = top + jnp.log(total)
    s = scores[...]
    weights, is_pos = masks(x_ref[0], ids[...], s.shape)
    d = (weights * jnp.exp(s - log_total) - is_pos).astype(jnp.bfloat16)
    wide = d.astype(jnp.float32)
    dscore[...] = d
    d_rows = jnp.transpose(wide).astype(jnp.bfloat16)
    ds = wide * s
    along_p = jnp.sum(ds, axis=1, keepdims=True)
    along_out[...] = along_p
    own = lax.broadcasted_iota(jnp.int32, (1, group_q), 1) < q_dev
    pos_score = jnp.sum(is_pos * s, axis=0, keepdims=True)
    value = jnp.sum(jnp.where(own, log_total - pos_score, 0.0))
    loss[...] = jnp.full(loss.shape, value, jnp.float32)
    pairs = jnp.exp(jnp.maximum(tops, pltpu.roll(tops, blocks - 1, 0)) - log_total)
    by = [pairs[j : j + 1] for j in range(0, blocks, 2)]
    by = columns(by + [jnp.sum(ds, axis=0, keepdims=True)])
    scales[...] = by[:q_dev]
    along_q = by[:, blocks // 2 : blocks // 2 + 1]

    for c in range(0, width, piece):
        cols = slice(c, c + piece)
        q, p = queries[:, cols], passages[:, cols]
        dq = logit_scale * jnp.dot(d_rows, p, preferred_element_type=jnp.float32)
        dq_own[:, cols] = dq[:q_dev]
        q, p = q.astype(jnp.float32), p.astype(jnp.float32)
        part = jnp.sum(q * (2.0 * dq - q * along_q), axis=0, keepdims=True)
        part = part - jnp.sum(p * (p * along_p), axis=0, keepdims=True)
        gain_part[:, cols] = part / gain[:, cols]


def grad_kernel(dscore, along, queries, hidden, gain, rms, length, grad_hbm, grad, sems):
    width = hidden.shape[1]
    r, inv, along_p = rms[...], length[...], along[...]
    d = dscore[...]
    by_dp = logit_scale * inv * r
    by_hg = inv * inv * r * r * along_p
    by_h = r * r * along_p * (inv * inv) * (len_eps / width)
    store = []
    for i, c in enumerate(range(0, width, piece)):
        cols = slice(c, c + piece)
        q, g = queries[:, cols], gain[:, cols]
        dp = jnp.dot(d, q, preferred_element_type=jnp.float32)
        h = hidden[:, cols].astype(jnp.float32)
        dnormed = by_dp * dp - by_hg * (h * g)
        grad[:, cols] = (dnormed * g - by_h * h).astype(jnp.bfloat16)
        done = pl.ds(c, piece)
        store.append(pltpu.make_async_copy(grad.at[:, done], grad_hbm.at[:, done], sems.at[i]))
        store[i].start()
    for copy in store:
        copy.wait()


def gain_sum_kernel(smalls, gain_grad, loss):
    small = smalls[0][...]
    for other in smalls[1:]:
        small = small + other[...]
    gain_grad[...] = small[:, : gain_grad.shape[1]]
    loss[...] = small[:, gain_grad.shape[1] : gain_grad.shape[1] + 1]


def query_grad_kernel(terms, dq_own, scales, hidden, gain, grad, dq):
    rows, width = hidden.shape
    r, inv = row_scales(hidden, gain, slice(0, 16))
    by = scales[...]
    along = jnp.zeros((rows, chunk), jnp.float32)
    for c in range(0, width, chunk):
        cols = slice(c, c + chunk)
        total = dq_own[:, cols]
        for j, term in enumerate(terms):
            total = total + term[:, cols].astype(jnp.float32) * by[:, j : j + 1]
        dq[:, cols] = total
        along = along + total * (hidden[:, cols].astype(jnp.float32) * gain[:, cols])
    along = jnp.sum(along, axis=1, keepdims=True) * (r * inv)
    mean = along * (inv * inv) * (len_eps / width)
    for c in range(0, width, chunk):
        cols = slice(c, c + chunk)
        h = hidden[:, cols].astype(jnp.float32)
        g = gain[:, cols]
        dnormed = inv * dq[:, cols] - (inv * inv * r * along) * (h * g)
        grad[:, cols] = (r * (dnormed * g) - (r * r * mean) * h).astype(jnp.bfloat16)


def on_device(n_dx, n_dy, query_hidden, passage_hidden, gain, hard_ids, positive_ids):
    q_dev, width = query_hidden.shape
    p_dev = passage_hidden.shape[0]
    group_q = n_dx * q_dev
    shape = jax.ShapeDtypeStruct
    bf16, f32 = jnp.bfloat16, jnp.float32
    gain = gain.reshape(1, width)
    x_index = lax.axis_index("dx").reshape(1)
    ids = jnp.concatenate([hard_ids, positive_ids[:, None]], axis=1).T
    ids = jnp.pad(ids, ((0, 0), (0, group_q - q_dev)), constant_values=-1)

    column, own = shape((p_dev, 1), f32), shape((q_dev, width), bf16)
    p_emb, p_rms, p_len, own_queries = call(
        embed_kernel, "embed", (shape((p_dev, width), bf16), column, column, own),
        (passage_hidden, query_hidden, gain), in_specs=[VMEM] * 3, out_specs=(VMEM,) * 4,
    )
    q_blocks, p_len = gather_blocks(query_hidden, "dx", n_dx, p_len)
    late = [j for j in range(n_dx) if j % 2 and j > 1]
    early = [j for j in range(1, n_dx) if j not in late]
    early_queries = call(
        lambda g, *refs: early_kernel(g, refs[:-1], refs[-1]), "early_queries",
        shape((len(early) * q_dev, width), bf16), (gain, *[q_blocks[j] for j in early]),
        in_specs=[VMEM] * (1 + len(early)), out_specs=VMEM,
    )
    macs = group_q * p_dev * width
    scores, stats, q_group = call(
        lambda x, i, p, g, o, e, *refs: score_kernel(
            early, late, x, i, p, g, o, e, refs[: len(late)], *refs[len(late) :]
        ), "scores",
        (shape((p_dev, group_q), f32), shape((2, 1, group_q), f32), shape((group_q, width), bf16)),
        (x_index, ids, p_emb, gain, own_queries, early_queries, *[q_blocks[j] for j in late]),
        flops=2 * macs, in_specs=[SMEM] + [VMEM] * (5 + len(late)), out_specs=(VMEM,) * 3,
    )
    half = n_dx // 4
    terms = shape((half, q_dev, width), bf16)
    stats = jnp.concatenate([stats, swap(stats, "dx", n_dx, 1)], axis=1)
    send_far, send_near, keep_far, keep_near = call(
        term_kernel, "query_terms", (terms,) * 4, (x_index, ids, stats, scores, p_emb),
        flops=2 * macs, in_specs=[SMEM] + [VMEM] * 4, out_specs=(VMEM,) * 4,
    )
    stats, send_far, send_near = lax.optimization_barrier((stats, send_far, send_near))
    far, near = swap(send_far, "dx", n_dx, 1), swap(send_near, "dx", n_dx, 1)
    stage = 2
    while stage < n_dx:
        stats = jnp.concatenate(spread(stats, "dx", n_dx, stage), axis=1)
        stage *= 4
    stats, far = lax.optimization_barrier((stats, far))
    far = far + keep_far
    far = [swap(far[i], "dx", n_dx, 2 * (half + i)) for i in range(half)]

    dscore, along, gain_part, dq_own, scales, loss = call(
        gain_kernel, "gain_part",
        (shape((p_dev, group_q), bf16), shape((p_dev, 1), f32), shape((1, width), f32),
         shape((q_dev, width), f32), shape((q_dev, 128), f32), shape((1, 128), f32)),
        (x_index, ids, stats, scores, q_group, p_emb, gain),
        flops=2 * macs, in_specs=[SMEM] + [VMEM] * 6, out_specs=(VMEM,) * 6,
    )
    passage_grad = call(
        grad_kernel, "passage_grad", shape((p_dev, width), bf16),
        (dscore, along, q_group, passage_hidden, gain, p_rms, p_len), flops=2 * macs,
        in_specs=[VMEM] * 7, out_specs=HBM,
        scratch_shapes=[pltpu.VMEM((p_dev, width), bf16),
                        pltpu.SemaphoreType.DMA((width // piece,))],
    )
    small = jnp.concatenate([gain_part, loss], axis=1)
    stage = 1
    while stage < n_dy:
        small = sum(spread(small, "dy", n_dy, stage))
        stage *= 4
    near, _ = lax.optimization_barrier((near, small))
    pairs = near + keep_near
    terms = [near[0]] + [swap(pairs[i], "dx", n_dx, 2 * i) for i in range(1, half)] + far
    bit = 1
    while 2 * bit < n_dx:
        small = small + swap(small, "dx", n_dx, bit)
        bit *= 2
    smalls = [small, swap(small, "dx", n_dx, bit)]
    n = len(terms)
    query_grad = call(
        lambda *refs: query_grad_kernel(refs[:n], *refs[n:]),
        "query_grad", shape((q_dev, width), bf16), (*terms, dq_own, scales, query_hidden, gain),
        in_specs=[VMEM] * (n + 4), out_specs=VMEM,
        scratch_shapes=[pltpu.VMEM((q_dev, width), f32)],
    )
    *smalls, _ = lax.optimization_barrier((*smalls, query_grad))
    gain_grad, loss = call(
        lambda *refs: gain_sum_kernel(refs[:-2], *refs[-2:]), "gain_sum",
        (shape((1, width), f32), shape((1, 1), f32)), smalls,
        in_specs=[VMEM] * len(smalls), out_specs=(VMEM,) * 2,
    )
    return (query_grad, passage_grad, gain_grad.reshape(width), loss.reshape(()))


def solution(mesh):
    n_dx, n_dy = mesh.shape["dx"], mesh.shape["dy"]
    placed = (
        P(("dx", "dy"), None),
        P(("dx", "dy"), None),
        P(),
        P(("dx", "dy"), None),
        P(("dx", "dy")),
    )
    return jax.shard_map(
        functools.partial(on_device, n_dx, n_dy),
        mesh=mesh,
        in_specs=placed,
        out_specs=(P(("dx", "dy"), None), P(("dx", "dy"), None), P(), P()),
        check_vma=False,
    )
```
